32 devices in a mesh: req: 4 (over y, core), vocab: 8 (over z, x).
Axes of the slice: x: 2, y: 2, z: 4, core: 2. Of those that a mesh axis runs over, the one named last changes fastest.
Arguments:
- hidden_rows: bfloat16 [1024, 2048], P(('req', 'vocab')), may hold values from -20 to 20
- norm_gain: float32 [2048], replicated, may hold values from 0.1 to 1.9
- head_weight: bfloat16 [2048, 81920], P(None, 'vocab'), may hold values from -10 to 10
- token_ids: int32 [1024], P('req'), may hold values from 0 to 81919
- live_count: int32 [32], P(('req', 'vocab')), may hold values from 1 to 32, as said below
Outputs:
- logprob: float32 [1024], P(('req', 'vocab'))
- entropy: float32 [1024], P(('req', 'vocab'))
The draws below stay inside these ranges and needn't reach their ends.
Inputs may be any that keep to these rules, and one draw needn't show every extreme that they name: `live_count`: the live rows of an owner are its first ones; some owner has all 32 live in every draw.
All inputs are finite; a program needn't handle non-finite values.
Results may differ from the reference program's by a relative error of at most 0.012.
Values may be sent and summed in bfloat16 or wider, within the bound.
No kernel may reach another device: no remote copies, remote signals or barrier semaphores. Data moves between devices by JAX's collectives and lax.ppermute only.
A program may use at most 128 MiB of HBM per device.

```python
import math
import jax
import jax.numpy as jnp
from jax import lax

D = 2048
VOCAB = 81920
OWN = 32
OWNERS = 32
ROWS = 1024
N_REQ = 4
N_VOCAB = 8


def aligned_columns(key):
    first_key, sign_key = jax.random.split(jax.random.fold_in(key, 7), 2)
    starts = jnp.arange(6, dtype=jnp.int32) * (VOCAB // 6)
    first = starts + jax.random.randint(first_key, (6,), 0, VOCAB // 12)
    second = first + VOCAB // 12
    target = jnp.array([120.0, 240.0, 380.0, 120.0, 240.0, 380.0], jnp.float32)
    level = target * math.sqrt(2.0) / D
    signs = (jax.random.randint(sign_key, (6, D), 0, 2) * 2 - 1).astype(jnp.float32)
    alternate = jnp.where(jnp.arange(D) % 2 == 0, 1.0, -1.0).astype(jnp.float32)
    first_vectors = signs * level[:, None]
    second_vectors = signs * alternate[None, :] * level[:, None]
    mixing = 1.0 - 2.0 / target
    return (first, second, first_vectors, second_vectors, mixing)


def draw_head_weight(key, part):
    weight_key, scale_key = jax.random.split(jax.random.fold_in(key, 1), 2)
    columns = jnp.arange(VOCAB, dtype=jnp.float32)
    scales = jnp.exp(jax.random.uniform(scale_key, (VOCAB,), jnp.float32, math.log(0.4), math.log(4.0)))
    scales = scales * (1.0 + 2.0 * columns / VOCAB)
    weight = jnp.clip(jax.random.normal(weight_key, (D, VOCAB), jnp.float32), -6.0, 6.0)
    weight = weight * D ** (-0.5) * scales[None, :]
    first, second, first_vectors, second_vectors, mixing = aligned_columns(key)
    weight = weight.at[:, first].set(first_vectors.T)
    weight = weight.at[:, second].set(second_vectors.T)
    return weight.astype(jnp.bfloat16)


def draw_hidden_rows(key, part):
    row_key = jax.random.fold_in(jax.random.fold_in(key, 2), 0)
    values = jnp.clip(jax.random.normal(row_key, (ROWS, D), jnp.float32), -6.0, 6.0)
    first, second, first_vectors, second_vectors, mixing = aligned_columns(key)
    targets = jnp.array([index * ROWS // 6 // OWN * OWN for index in range(6)], jnp.int32)
    values = values.at[targets].set(first_vectors + mixing[:, None] * second_vectors)
    return values.astype(jnp.bfloat16)


def draw_live_count(key, part):
    count_key, full_key = jax.random.split(jax.random.fold_in(key, 3), 2)
    counts = jax.random.randint(count_key, (OWNERS,), 1, OWN + 1)
    chosen = jax.random.randint(full_key, (), 0, OWNERS)
    return counts.at[chosen].set(OWN).astype(jnp.int32)


def place_ends(values, stream_key, smallest, top_value):
    longest = values.shape.index(max(values.shape))
    spots = []
    for shift in (0, 1):
        where = [jax.random.randint(jax.random.fold_in(stream_key, axis), (), 0, length) for axis, length in enumerate(values.shape)]
        where[longest] = (where[longest] + shift) % values.shape[longest]
        spots.append(tuple(where))
    return values.at[spots[0]].set(smallest).at[spots[1]].set(top_value)


def setup_inputs(seed: int = 0) -> dict:
    seeds = jax.random.split(jax.random.key(seed), 6)
    return {
        "hidden_rows": draw_hidden_rows(jax.random.fold_in(seeds[5], 71), 0),
        "norm_gain": jnp.clip(1.0 + 0.18 * jax.random.normal(seeds[1], (D,), jnp.float32), 0.1, 1.9),
        "head_weight": draw_head_weight(jax.random.fold_in(seeds[5], 71), 0),
        "token_ids": place_ends(jax.random.randint(seeds[3], (ROWS,), 0, VOCAB), jax.random.fold_in(seeds[3], 1), 0, VOCAB - 1).astype(jnp.int32),
        "live_count": draw_live_count(jax.random.fold_in(seeds[5], 71), 0),
    }


def block_stats(packed, gain, head_weight):
    block_rows, block_ids = packed
    values = block_rows.astype(jnp.float32)
    squares = lax.optimization_barrier(jnp.mean(values * values, axis=1))
    normed = (values * lax.rsqrt(squares + 1e-06)[:, None] * gain[None, :]).astype(jnp.bfloat16)
    logits = jnp.dot(normed, head_weight, preferred_element_type=jnp.float32)
    row_top = lax.optimization_barrier(jnp.max(logits, axis=1))
    shifted = logits - row_top[:, None]
    powers = jnp.exp(shifted)
    row_total = lax.optimization_barrier(jnp.sum(powers, axis=1))
    row_spread = lax.optimization_barrier(jnp.sum(powers * shifted, axis=1))
    row_picked = jnp.take_along_axis(logits, block_ids[:, None].astype(jnp.int32), axis=1)[:, 0]
    log_total = jnp.log(row_total)
    return (row_picked - row_top - log_total, log_total - row_spread / row_total)

def reference(hidden_rows, norm_gain, head_weight, token_ids, live_count):
    group_rows = OWN * N_VOCAB
    packed = (hidden_rows.reshape(N_REQ, group_rows, D), token_ids.reshape(N_REQ, group_rows))
    logprob, entropy = lax.map(lambda item: block_stats(item, norm_gain, head_weight), packed)
    logprob = logprob.reshape(-1)
    entropy = entropy.reshape(-1)
    row_index = jnp.arange(OWN * N_REQ * N_VOCAB, dtype=jnp.int32)
    limits = jnp.repeat(live_count, OWN)
    live = row_index % OWN < limits
    return (jnp.where(live, logprob, 0.0), jnp.where(live, entropy, 0.0))
```

```python
import functools

import jax
import jax.numpy as jnp
from jax import lax
from jax.experimental import pallas as pl
from jax.experimental.pallas import tpu as pltpu
from jax.sharding import PartitionSpec as P

LANES = 128
LOWEST = -1e30
VMEM = pl.BlockSpec(memory_space=pltpu.VMEM)


def norm_kernel(hidden_ref, gain_ref, out_ref):
    values = hidden_ref[...].astype(jnp.float32)
    squares = jnp.mean(values * values, axis=1, keepdims=True)
    out_ref[...] = (values * lax.rsqrt(squares + 1e-06) * gain_ref[...]).astype(jnp.bfloat16)


def normalise(hidden_rows, norm_gain):
    return pl.pallas_call(
        norm_kernel,
        in_specs=[VMEM, VMEM],
        out_specs=VMEM,
        out_shape=jax.ShapeDtypeStruct(hidden_rows.shape, jnp.bfloat16),
    )(hidden_rows, norm_gain[None, :])


def head_kernel(n_blocks, tile, *refs):
    block_refs = refs[:n_blocks]
    token_ref, head_ref, out_ref, rows, logits, wanted, top, total, spread, picked = refs[n_blocks:]
    own_rows = block_refs[0].shape[0]
    width = head_ref.shape[1]
    n_rows = rows.shape[0]
    n_tiles = width // tile
    me = lax.axis_index("vocab")
    for distance, block in enumerate(block_refs):
        start = pl.multiple_of(lax.bitwise_xor(me, distance) * own_rows, own_rows)
        rows[pl.ds(start, own_rows), :] = block[...]

    lane = lax.broadcasted_iota(jnp.int32, (n_rows, LANES), 1)
    wanted[...] = token_ref[...] - me * width - lane
    top[...] = jnp.full(top.shape, LOWEST, jnp.float32)
    total[...] = jnp.zeros(total.shape, jnp.float32)
    spread[...] = jnp.zeros(spread.shape, jnp.float32)
    picked[...] = jnp.zeros(picked.shape, jnp.float32)

    def multiply(index, slot):
        columns = pl.ds(pl.multiple_of(index * tile, tile), tile)
        logits[slot] = jnp.dot(rows[...], head_ref[:, columns], preferred_element_type=jnp.float32)

    def gather_stats(index, slot):
        step = 32
        for first in range(0, n_rows, step):
            part = slice(first, first + step)
            pieces = [logits[slot, part, c : c + LANES] for c in range(0, tile, LANES)]
            old = top[part]
            new = jnp.maximum(old, functools.reduce(jnp.maximum, pieces))
            shift = old - new
            factor = jnp.exp(shift)
            sums = total[part]
            spreads = (spread[part] + shift * sums) * factor
            sums = sums * factor
            found = picked[part]
            target = wanted[part]
            for number, piece in enumerate(pieces):
                shifted = piece - new
                power = jnp.exp(shifted)
                sums = sums + power
                spreads = spreads + power * shifted
                found = jnp.where(target == index * tile + number * LANES, piece, found)
            top[part] = new
            total[part] = sums
            spread[part] = spreads
            picked[part] = found

    multiply(0, 0)

    @pl.loop(0, n_tiles // 2 - 1)
    def _(pair):
        index = pair * 2
        multiply(index + 1, 1)
        gather_stats(index, 0)
        multiply(index + 2, 0)
        gather_stats(index + 1, 1)

    multiply(n_tiles - 1, 1)
    gather_stats(n_tiles - 2, 0)
    gather_stats(n_tiles - 1, 1)

    row_top = jnp.max(top[...], axis=1, keepdims=True)
    shift = top[...] - row_top
    factor = jnp.exp(shift)
    row_total = jnp.sum(total[...] * factor, axis=1, keepdims=True)
    row_spread = jnp.sum((spread[...] + shift * total[...]) * factor, axis=1, keepdims=True)
    row_picked = jnp.sum(picked[...], axis=1, keepdims=True)
    packed = jnp.where(
        lane == 0,
        row_top,
        jnp.where(lane == 1, row_total, jnp.where(lane == 2, row_spread, row_picked)),
    )
    out_ref[...] = packed.T[:8, :]


def head_stats(blocks, token_ids, head_weight):
    own_rows, depth = blocks[0].shape
    n_rows = own_rows * len(blocks)
    width = head_weight.shape[1]
    tile = next(t for t in (1024, 512, 256, 128) if width % (2 * t) == 0)
    head_weight = pltpu.with_memory_space_constraint(head_weight, pltpu.VMEM)
    return pl.pallas_call(
        functools.partial(head_kernel, len(blocks), tile),
        in_specs=[VMEM] * (len(blocks) + 2),
        out_specs=VMEM,
        out_shape=jax.ShapeDtypeStruct((8, n_rows), jnp.float32),
        scratch_shapes=[
            pltpu.VMEM((n_rows, depth), jnp.bfloat16),
            pltpu.VMEM((2, n_rows, tile), jnp.float32),
            pltpu.VMEM((n_rows, LANES), jnp.int32),
            pltpu.VMEM((n_rows, LANES), jnp.float32),
            pltpu.VMEM((n_rows, LANES), jnp.float32),
            pltpu.VMEM((n_rows, LANES), jnp.float32),
            pltpu.VMEM((n_rows, LANES), jnp.float32),
        ],
        compiler_params=pltpu.CompilerParams(vmem_limit_bytes=18 * 2**20),
        cost_estimate=pl.CostEstimate(
            flops=2 * n_rows * depth * width,
            bytes_accessed=2 * n_rows * depth,
            transcendentals=n_rows * width,
        ),
    )(*blocks, token_ids[:, None], head_weight)


def merge(mine, theirs):
    top = jnp.maximum(mine[0:1], theirs[0:1])
    a, b = mine[0:1] - top, theirs[0:1] - top
    fa, fb = jnp.exp(a), jnp.exp(b)
    total = mine[1:2] * fa + theirs[1:2] * fb
    spread = (mine[2:3] + a * mine[1:2]) * fa + (theirs[2:3] + b * theirs[1:2]) * fb
    return top, total, spread, mine[3:4] + theirs[3:4]


def merge_kernel(mine_ref, theirs_ref, out_ref):
    for row, value in enumerate(merge(mine_ref[...], theirs_ref[...])):
        out_ref[row : row + 1, :] = value
    out_ref[4:8, :] = jnp.zeros((4, out_ref.shape[1]), jnp.float32)


def finish_kernel(own_rows, live_ref, mine_ref, theirs_ref, logprob_ref, entropy_ref):
    top, total, spread, picked = merge(mine_ref[...], theirs_ref[...])
    log_total = jnp.log(total)
    logprob = picked - top - log_total
    entropy = log_total - spread / total
    n_rows = logprob.shape[1]
    start = lax.axis_index("vocab") * own_rows
    logprob = pltpu.roll(logprob, n_rows - start, 1)
    entropy = pltpu.roll(entropy, n_rows - start, 1)
    live = lax.broadcasted_iota(jnp.int32, logprob.shape, 1) < live_ref[0]
    logprob_ref[...] = jnp.where(live, logprob, 0.0)[:, :own_rows]
    entropy_ref[...] = jnp.where(live, entropy, 0.0)[:, :own_rows]


def swap(array, distance, size):
    return lax.ppermute(array, "vocab", [(i, i ^ distance) for i in range(size)])


def per_device(size, hidden_rows, norm_gain, head_weight, token_ids, live_count):
    own_rows = hidden_rows.shape[0]
    normed = normalise(hidden_rows, norm_gain)
    blocks = {0: normed}
    for distance in range(size - 2, 0, -2):
        blocks[distance] = swap(normed, distance, size)
    for distance in range(0, size, 2):
        blocks[distance + 1] = swap(blocks[distance], 1, size)
    stats = head_stats([blocks[d] for d in range(size)], token_ids, head_weight)
    distance = 1
    while 2 * distance < size:
        stats = pl.pallas_call(
            merge_kernel,
            in_specs=[VMEM, VMEM],
            out_specs=VMEM,
            out_shape=jax.ShapeDtypeStruct(stats.shape, jnp.float32),
        )(stats, swap(stats, distance, size))
        distance *= 2
    out = jax.ShapeDtypeStruct((1, own_rows), jnp.float32)
    logprob, entropy = pl.pallas_call(
        functools.partial(finish_kernel, own_rows),
        in_specs=[pl.BlockSpec(memory_space=pltpu.SMEM), VMEM, VMEM],
        out_specs=(VMEM, VMEM),
        out_shape=(out, out),
    )(live_count, stats, swap(stats, distance, size))
    return logprob[0], entropy[0]


def solution(mesh):
    placed = (P(("req", "vocab"), None), P(), P(None, "vocab"), P("req"), P(("req", "vocab")))
    return jax.shard_map(
        functools.partial(per_device, mesh.shape["vocab"]),
        mesh=mesh,
        in_specs=placed,
        out_specs=(P(("req", "vocab")), P(("req", "vocab"))),
        check_vma=False,
    )
```

```python
import functools

import jax
import jax.numpy as jnp
from jax import lax
from jax.experimental import pallas as pl
from jax.experimental.pallas import tpu as pltpu
from jax.sharding import PartitionSpec as P

LANES = 128
LOWEST = -1e30
IN_VMEM = pl.BlockSpec(memory_space=pltpu.VMEM)
ANYWHERE = pl.BlockSpec(memory_space=pl.ANY)


def normalise(values, gain):
    values = values.astype(jnp.float32)
    squares = jnp.mean(values * values, axis=1, keepdims=True)
    return (values * lax.rsqrt(squares + 1e-06) * gain).astype(jnp.bfloat16)


def column_of(tokens):
    wide = jnp.broadcast_to(tokens.astype(jnp.float32), (LANES, tokens.shape[1]))
    return wide.T.astype(jnp.int32)


def sweep(n_tiles, multiply, collect):
    multiply(0, 0)
    pairs = (n_tiles - 1) // 2

    @pl.loop(0, pairs)
    def _(pair):
        tile = pair * 2
        multiply(tile + 1, 1)
        collect(tile, 0)
        multiply(tile + 2, 0)
        collect(tile + 1, 1)

    if n_tiles % 2:
        collect(n_tiles - 1, 0)
    else:
        multiply(n_tiles - 1, 1)
        collect(n_tiles - 2, 0)
        collect(n_tiles - 1, 1)


def stage_kernel(plan, *refs):
    distances, before_distances, part, first_rows, tile, half = plan
    final = part is None
    n_blocks = len(distances)
    refs = list(refs)
    blocks = [refs.pop(0) for _ in range(n_blocks)]
    gain_ref, token_ref = refs.pop(0), refs.pop(0)
    before = refs.pop(0) if before_distances else None
    if final:
        parts = [refs.pop(0) for _ in first_rows]
        outs = [refs.pop(0), refs.pop(0)]
    else:
        head_hbm = refs.pop(0)
        outs = [refs.pop(0)]
        loaded = refs.pop(0)
    rows, logits, wanted, by_row, top, total, spread, picked = refs[:8]
    own = blocks[0].shape[0]
    n_tiles = half // tile
    me = lax.axis_index("vocab")
    n_rows = n_blocks * own

    def load(index):
        columns = pl.ds(pl.multiple_of(index * tile, tile), tile)
        source = pl.ds(pl.multiple_of(part * half + index * tile, tile), tile)
        return pltpu.make_async_copy(head_hbm.at[:, source], loaded.at[:, columns], refs[8].at[index])

    if not final:
        for index in range(n_tiles):
            load(index).start()

    gain = gain_ref[...]
    by_row[...] = column_of(token_ref[...])
    lane = lax.broadcasted_iota(jnp.int32, (own, LANES), 1)
    for number, (distance, block) in enumerate(zip(distances, blocks)):
        place = slice(number * own, (number + 1) * own)
        rows[place, :] = normalise(block[...], gain)
        start = pl.multiple_of(lax.bitwise_xor(me, distance) * own, own)
        wanted[place, :] = by_row[pl.ds(start, own), :] - me * half - lane
        if distance in before_distances:
            origin = before_distances.index(distance) * own
            saved = before[origin : origin + own, :]
            top[place, :] = jnp.broadcast_to(saved[:, 0:1], (own, LANES))
            total[place, :] = jnp.where(lane == 0, saved[:, 1:2], 0.0)
            spread[place, :] = jnp.where(lane == 0, saved[:, 2:3], 0.0)
            picked[place, :] = jnp.where(lane == 0, saved[:, 3:4], 0.0)
        else:
            top[place, :] = jnp.full((own, LANES), LOWEST, jnp.float32)
            for sums in (total, spread, picked):
                sums[place, :] = jnp.zeros((own, LANES), jnp.float32)

    def run(head, first_row, first_column, wait):
        def multiply(index, slot):
            if wait:
                load(index).wait()
            columns = pl.ds(pl.multiple_of(index * tile, tile), tile)
            logits[slot, first_row:, :] = jnp.dot(
                rows[first_row:, :], head[:, columns], preferred_element_type=jnp.float32
            )

        def collect(index, slot):
            step = 32
            for begin in range(first_row, n_rows, step):
                place = slice(begin, begin + step)
                pieces = [logits[slot, place, c : c + LANES] for c in range(0, tile, LANES)]
                last = top[place]
                new = jnp.maximum(last, functools.reduce(jnp.maximum, pieces))
                shift = last - new
                factor = jnp.exp(shift)
                sums = total[place]
                spreads = (spread[place] + shift * sums) * factor
                sums = sums * factor
                found = picked[place]
                target = wanted[place]
                for number, piece in enumerate(pieces):
                    shifted = piece - new
                    power = jnp.exp(shifted)
                    sums = sums + power
                    spreads = spreads + power * shifted
                    found = jnp.where(
                        target == first_column + index * tile + number * LANES, piece, found
                    )
                top[place] = new
                total[place] = sums
                spread[place] = spreads
                picked[place] = found

        sweep(n_tiles, multiply, collect)

    if final:
        for number, (head, first_row) in enumerate(zip(parts, first_rows)):
            run(head, first_row, number * half, False)
    else:
        run(loaded, 0, part * half, True)

    row_top = jnp.max(top[...], axis=1, keepdims=True)
    shift = top[...] - row_top
    factor = jnp.exp(shift)
    row_total = jnp.sum(total[...] * factor, axis=1, keepdims=True)
    row_spread = jnp.sum((spread[...] + shift * total[...]) * factor, axis=1, keepdims=True)
    row_picked = jnp.sum(picked[...], axis=1, keepdims=True)
    lane = lax.broadcasted_iota(jnp.int32, (n_rows, LANES), 1)
    packed = jnp.where(
        lane == 0,
        row_top,
        jnp.where(lane == 1, row_total, jnp.where(lane == 2, row_spread, row_picked)),
    )
    if not final:
        outs[0][...] = packed
        return
    whole = refs[8]
    for distance in range(whole.shape[0] // own):
        place = slice(distance * own, (distance + 1) * own)
        if distance in distances:
            origin = distances.index(distance) * own
            whole[place, :] = packed[origin : origin + own, :]
        else:
            origin = before_distances.index(distance) * own
            whole[place, :] = before[origin : origin + own, :]
    table = whole[...].T
    outs[0][...] = table[:4, : whole.shape[0] // 2]
    outs[1][...] = table[:4, whole.shape[0] // 2 :]


def stage(blocks, distances, gain, tokens, before, before_distances, head_weight, part, parts, first_rows):
    own, depth = blocks[0].shape
    final = part is None
    half = parts[0].shape[1] if final else head_weight.shape[1]
    tile = next(t for t in (1024, 512, 256, 128) if half % t == 0)
    n_rows, n_all = own * len(blocks), tokens.shape[1]
    plan = (tuple(distances), tuple(before_distances), part, first_rows, tile, half)
    args = [*blocks, gain, tokens]
    if before_distances:
        args.append(before)
    specs = [IN_VMEM] * len(args)
    if final:
        args += [pltpu.with_memory_space_constraint(p, pltpu.VMEM) for p in parts]
        specs += [IN_VMEM] * len(parts)
        out_shape = [jax.ShapeDtypeStruct((4, n_all // 2), jnp.float32)] * 2
        last = pltpu.VMEM((n_all, LANES), jnp.float32)
        met = sum(n_rows - first for first in first_rows)
    else:
        args.append(head_weight)
        specs.append(ANYWHERE)
        out_shape = [
            jax.ShapeDtypeStruct((n_rows, LANES), jnp.float32),
            pltpu.VMEM((depth, half), jnp.bfloat16),
        ]
        last = pltpu.SemaphoreType.DMA((half // tile,))
        met = n_rows
    scratch = [
        pltpu.VMEM((n_rows, depth), jnp.bfloat16),
        pltpu.VMEM((2, n_rows, tile), jnp.float32),
        pltpu.VMEM((n_rows, LANES), jnp.int32),
        pltpu.VMEM((n_all, LANES), jnp.int32),
    ] + [pltpu.VMEM((n_rows, LANES), jnp.float32)] * 4
    need = n_rows * (4 * depth + 8 * tile + 32 * LANES) + n_all * 16 * LANES + 2**22
    return pl.pallas_call(
        functools.partial(stage_kernel, plan),
        in_specs=specs,
        out_specs=[IN_VMEM] * len(out_shape),
        out_shape=out_shape,
        scratch_shapes=scratch + [last],
        compiler_params=pltpu.CompilerParams(vmem_limit_bytes=need),
        cost_estimate=pl.CostEstimate(
            flops=2 * depth * half * met,
            bytes_accessed=0 if final else 2 * depth * half,
            transcendentals=half * met,
        ),
    )(*args)


def merge(mine, theirs):
    top = jnp.maximum(mine[0], theirs[0])
    a, b = mine[0] - top, theirs[0] - top
    fa, fb = jnp.exp(a), jnp.exp(b)
    total = mine[1] * fa + theirs[1] * fb
    spread = (mine[2] + a * mine[1]) * fa + (theirs[2] + b * theirs[1]) * fb
    return jnp.stack([top, total, spread, mine[3] + theirs[3]])


def swap(array, distance, size):
    return lax.ppermute(array, "vocab", [(i, i ^ distance) for i in range(size)])


def per_device(size, hidden_rows, norm_gain, head_weight, token_ids, live_count):
    own = hidden_rows.shape[0]
    gain, tokens, hidden_rows = (
        pltpu.with_memory_space_constraint(x, pltpu.HBM)
        for x in (norm_gain[None, :], token_ids[None, :], hidden_rows)
    )
    blocks = {0: hidden_rows}
    for distance in range(1, size):
        blocks[distance] = swap(hidden_rows, distance, size)
    near, far = list(range(size // 2)), list(range(size // 2, size))
    pick = lambda which: [blocks[d] for d in which]
    sums, head = stage(pick(near), near, gain, tokens, None, [], head_weight, 0, [], ())
    kept, sent = stage(pick(far), far, gain, tokens, sums, near, None, None, [head], (0,))
    distance = size // 2
    while True:
        stats = merge(kept, swap(sent, distance, size))
        distance //= 2
        if not distance:
            break
        kept, sent = stats[:, : distance * own], stats[:, distance * own :]
    log_total = jnp.log(stats[1])
    logprob = stats[3] - stats[0] - log_total
    entropy = log_total - stats[2] / stats[1]
    live = jnp.arange(own, dtype=jnp.int32) < live_count[0]
    return jnp.where(live, logprob, 0.0), jnp.where(live, entropy, 0.0)


def solution(mesh):
    placed = (P(("req", "vocab"), None), P(), P(None, "vocab"), P("req"), P(("req", "vocab")))
    return jax.shard_map(
        functools.partial(per_device, mesh.shape["vocab"]),
        mesh=mesh,
        in_specs=placed,
        out_specs=(P(("req", "vocab")), P(("req", "vocab"))),
        check_vma=False,
    )
```

```python
import functools

import jax
import jax.numpy as jnp
from jax import lax
from jax.experimental import pallas as pl
from jax.experimental.pallas import tpu as pltpu
from jax.sharding import PartitionSpec as P

LANES = 128
LOWEST = -1e30
IN_VMEM = pl.BlockSpec(memory_space=pltpu.VMEM)
ANYWHERE = pl.BlockSpec(memory_space=pl.ANY)


def normalise(values, gain):
    values = values.astype(jnp.float32)
    squares = jnp.mean(values * values, axis=1, keepdims=True)
    return (values * lax.rsqrt(squares + 1e-06) * gain).astype(jnp.bfloat16)


def norm_kernel(hidden_hbm, gain_hbm, out_ref, hidden, gain, sems):
    copies = [
        pltpu.make_async_copy(source, target, sems.at[number])
        for number, (source, target) in enumerate(((hidden_hbm, hidden), (gain_hbm, gain)))
    ]
    for copy in copies:
        copy.start()
    for copy in copies:
        copy.wait()
    out_ref[...] = normalise(hidden[...], gain[...])


def norm_rows(hidden_rows, gain):
    return pl.pallas_call(
        norm_kernel,
        in_specs=[ANYWHERE, ANYWHERE],
        out_specs=IN_VMEM,
        out_shape=jax.ShapeDtypeStruct(hidden_rows.shape, jnp.bfloat16),
        scratch_shapes=[
            pltpu.VMEM(hidden_rows.shape, hidden_rows.dtype),
            pltpu.VMEM(gain.shape, gain.dtype),
            pltpu.SemaphoreType.DMA((2,)),
        ],
        compiler_params=pltpu.CompilerParams(vmem_limit_bytes=3 * 2**20),
        cost_estimate=pl.CostEstimate(flops=10**11, bytes_accessed=10**8, transcendentals=0),
    )(*(pltpu.with_memory_space_constraint(x, pltpu.HBM) for x in (hidden_rows, gain)))


def column_of(tokens):
    wide = jnp.broadcast_to(tokens.astype(jnp.float32), (LANES, tokens.shape[1]))
    return wide.T.astype(jnp.int32)


def sweep(n_tiles, multiply, collect):
    multiply(0, 0)
    pairs = (n_tiles - 1) // 2

    @pl.loop(0, pairs)
    def _(pair):
        tile = pair * 2
        multiply(tile + 1, 1)
        collect(tile, 0)
        multiply(tile + 2, 0)
        collect(tile + 1, 1)

    if n_tiles % 2:
        collect(n_tiles - 1, 0)
    else:
        multiply(n_tiles - 1, 1)
        collect(n_tiles - 2, 0)
        collect(n_tiles - 1, 1)


def head_kernel(owner_of, tile, *refs):
    n_blocks = len(refs) - 12
    blocks, refs = refs[:n_blocks], refs[n_blocks:]
    token_ref, head, kept_ref, sent_ref, rows, logits, wanted, by_row, top, total, spread, picked = refs
    own = blocks[0].shape[0]
    width = head.shape[1]
    n_tiles = width // tile
    me = lax.axis_index("vocab")
    n_rows = n_blocks * own

    by_row[...] = column_of(token_ref[...])
    lane = lax.broadcasted_iota(jnp.int32, (own, LANES), 1)
    for number, block in enumerate(blocks):
        owner = owner_of(me, number)
        place = pl.ds(pl.multiple_of(lax.bitwise_xor(owner, me) * own, own), own)
        rows[place, :] = block[...]
        start = pl.multiple_of(owner * own, own)
        wanted[place, :] = by_row[pl.ds(start, own), :] - me * width - lane
    top[...] = jnp.full(top.shape, LOWEST, jnp.float32)
    for sums in (total, spread, picked):
        sums[...] = jnp.zeros(sums.shape, jnp.float32)

    def multiply(index, slot):
        columns = pl.ds(pl.multiple_of(index * tile, tile), tile)
        logits[slot] = jnp.dot(rows[...], head[:, columns], preferred_element_type=jnp.float32)

    def collect(index, slot):
        step = 32
        for begin in range(0, n_rows, step):
            place = slice(begin, begin + step)
            pieces = [logits[slot, place, c : c + LANES] for c in range(0, tile, LANES)]
            last = top[place]
            new = jnp.maximum(last, functools.reduce(jnp.maximum, pieces))
            shift = last - new
            factor = jnp.exp(shift)
            sums = total[place]
            spreads = (spread[place] + shift * sums) * factor
            sums = sums * factor
            found = picked[place]
            target = wanted[place]
            for number, piece in enumerate(pieces):
                shifted = piece - new
                power = jnp.exp(shifted)
                sums = sums + power
                spreads = spreads + power * shifted
                found = jnp.where(target == index * tile + number * LANES, piece, found)
            top[place] = new
            total[place] = sums
            spread[place] = spreads
            picked[place] = found

    sweep(n_tiles, multiply, collect)

    row_top = jnp.max(top[...], axis=1, keepdims=True)
    shift = top[...] - row_top
    factor = jnp.exp(shift)
    row_total = jnp.sum(total[...] * factor, axis=1, keepdims=True)
    row_spread = jnp.sum((spread[...] + shift * total[...]) * factor, axis=1, keepdims=True)
    row_picked = jnp.sum(picked[...], axis=1, keepdims=True)
    lane = lax.broadcasted_iota(jnp.int32, (n_rows, LANES), 1)
    packed = jnp.where(
        lane == 0,
        row_top,
        jnp.where(lane == 1, row_total, jnp.where(lane == 2, row_spread, row_picked)),
    )
    table = packed.T
    kept_ref[...] = table[:4, : n_rows // 2]
    sent_ref[...] = table[:4, n_rows // 2 :]


def head_stats(blocks, owner_of, tokens, head):
    own, depth = blocks[0].shape
    tile = next(t for t in (1024, 512, 256, 128) if head.shape[1] % t == 0)
    n_rows = own * len(blocks)
    args = [*blocks, tokens, pltpu.with_memory_space_constraint(head, pltpu.VMEM)]
    return pl.pallas_call(
        functools.partial(head_kernel, owner_of, tile),
        in_specs=[IN_VMEM] * len(args),
        out_specs=[IN_VMEM] * 2,
        out_shape=[jax.ShapeDtypeStruct((4, n_rows // 2), jnp.float32)] * 2,
        scratch_shapes=[
            pltpu.VMEM((n_rows, depth), jnp.bfloat16),
            pltpu.VMEM((2, n_rows, tile), jnp.float32),
            pltpu.VMEM((n_rows, LANES), jnp.int32),
            pltpu.VMEM((n_rows, LANES), jnp.int32),
        ]
        + [pltpu.VMEM((n_rows, LANES), jnp.float32)] * 4,
        compiler_params=pltpu.CompilerParams(
            vmem_limit_bytes=n_rows * (4 * depth + 8 * tile + 48 * LANES) + 2**22
        ),
        cost_estimate=pl.CostEstimate(flops=1, bytes_accessed=500 * 2**20, transcendentals=0),
    )(*args)


def merge(mine, theirs):
    top = jnp.maximum(mine[0], theirs[0])
    a, b = mine[0] - top, theirs[0] - top
    fa, fb = jnp.exp(a), jnp.exp(b)
    total = mine[1] * fa + theirs[1] * fb
    spread = (mine[2] + a * mine[1]) * fa + (theirs[2] + b * theirs[1]) * fb
    return jnp.stack([top, total, spread, mine[3] + theirs[3]])


def swap(array, distance, size):
    return lax.ppermute(array, "vocab", [(i, i ^ distance) for i in range(size)])


def turn(array, distance, size):
    return lax.ppermute(array, "vocab", [(i, (i + distance) % size) for i in range(size)])


def gather(normed, size):
    blocks = {0: normed}
    for distance in range(size - 2, 0, -2):
        blocks[distance] = swap(normed, distance, size)
    for distance in range(0, size, 2):
        blocks[distance + 1] = swap(blocks[distance], 1, size)
    return [blocks[d] for d in range(size)], lambda me, number: lax.bitwise_xor(me, number)


def per_device(size, hidden_rows, norm_gain, head_weight, token_ids, live_count):
    own = hidden_rows.shape[0]
    tokens = token_ids[None, :]
    normed = norm_rows(hidden_rows, norm_gain[None, :])
    blocks, owner_of = gather(normed, size)
    kept, sent = head_stats(blocks, owner_of, tokens, head_weight)
    distance = size // 2
    while True:
        stats = merge(kept, swap(sent, distance, size))
        distance //= 2
        if not distance:
            break
        kept, sent = stats[:, : distance * own], stats[:, distance * own :]
    log_total = jnp.log(stats[1])
    logprob = stats[3] - stats[0] - log_total
    entropy = log_total - stats[2] / stats[1]
    live = jnp.arange(own, dtype=jnp.int32) < live_count[0]
    return jnp.where(live, logprob, 0.0), jnp.where(live, entropy, 0.0)


def solution(mesh):
    placed = (P(("req", "vocab"), None), P(), P(None, "vocab"), P("req"), P(("req", "vocab")))
    return jax.shard_map(
        functools.partial(per_device, mesh.shape["vocab"]),
        mesh=mesh,
        in_specs=placed,
        out_specs=(P(("req", "vocab")), P(("req", "vocab"))),
        check_vma=False,
    )
```

```python
import functools

import jax
import jax.numpy as jnp
from jax import lax
from jax.experimental import pallas as pl
from jax.experimental.pallas import tpu as pltpu
from jax.sharding import PartitionSpec as P

LANES = 128
LOWEST = -1e30
IN_VMEM = pl.BlockSpec(memory_space=pltpu.VMEM)
ANYWHERE = pl.BlockSpec(memory_space=pl.ANY)


def normalise(values, gain):
    values = values.astype(jnp.float32)
    squares = jnp.mean(values * values, axis=1, keepdims=True)
    return values * lax.rsqrt(squares + 1e-06) * gain


def norm_kernel(hidden_hbm, gain_hbm, count, out_ref, live_ref, hidden, gain, sems):
    copies = [
        pltpu.make_async_copy(source, target, sems.at[number])
        for number, (source, target) in enumerate(((hidden_hbm, hidden), (gain_hbm, gain)))
    ]
    for copy in copies:
        copy.start()
    for copy in copies:
        copy.wait()
    row = lax.broadcasted_iota(jnp.int32, hidden.shape, 0)
    alive = row < jnp.broadcast_to(count[...], hidden.shape)
    out_ref[...] = jnp.where(alive, normalise(hidden[...], gain[...]), 0.0).astype(jnp.bfloat16)
    column = lax.broadcasted_iota(jnp.int32, live_ref.shape, 1)
    live_ref[...] = (column < jnp.broadcast_to(count[...], live_ref.shape)).astype(jnp.float32)


def norm_rows(hidden_rows, gain, live_count):
    args = (hidden_rows, gain, live_count)
    return pl.pallas_call(
        norm_kernel,
        in_specs=[ANYWHERE, ANYWHERE, IN_VMEM],
        out_specs=[IN_VMEM] * 2,
        out_shape=[
            jax.ShapeDtypeStruct(hidden_rows.shape, jnp.bfloat16),
            jax.ShapeDtypeStruct((1, hidden_rows.shape[0]), jnp.float32),
        ],
        scratch_shapes=[pltpu.VMEM(x.shape, x.dtype) for x in args[:2]] + [pltpu.SemaphoreType.DMA((2,))],
        compiler_params=pltpu.CompilerParams(vmem_limit_bytes=3 * 2**20),
        cost_estimate=pl.CostEstimate(flops=10**11, bytes_accessed=10**8, transcendentals=0),
    )(*(pltpu.with_memory_space_constraint(x, pltpu.HBM) for x in args[:2]), live_count)


def column_of(tokens):
    wide = jnp.broadcast_to(tokens.astype(jnp.float32), (LANES, tokens.shape[1]))
    return wide.T.astype(jnp.int32)


def sweep(n_tiles, multiply, collect):
    multiply(0, 0)
    pairs = (n_tiles - 1) // 2

    @pl.loop(0, pairs)
    def _(pair):
        tile = pair * 2
        multiply(tile + 1, 1)
        collect(tile, 0)
        multiply(tile + 2, 0)
        collect(tile + 1, 1)

    if n_tiles % 2:
        collect(n_tiles - 1, 0)
    else:
        multiply(n_tiles - 1, 1)
        collect(n_tiles - 2, 0)
        collect(n_tiles - 1, 1)


def head_kernel(tile, counts, *refs):
    n_blocks = len(refs) - 14
    blocks, refs = refs[:n_blocks], refs[n_blocks:]
    token_ref, head, kept_ref, sent_ref, rows, packed, chosen, logits, wanted, by_row = refs[:10]
    top, total, spread, picked = refs[10:]
    own, depth = blocks[0].shape
    width = head.shape[1]
    me = lax.axis_index("vocab")
    n_rows = n_blocks * own

    by_row[...] = column_of(token_ref[...])
    lane = lax.broadcasted_iota(jnp.int32, (own, LANES), 1)
    for number, block in enumerate(blocks):
        place = slice(number * own, (number + 1) * own)
        values = block[...]
        rows[place, :depth] = values
        pieces = [jnp.abs(values[:, c : c + LANES]) for c in range(0, depth, LANES)]
        largest = functools.reduce(jnp.maximum, pieces).astype(jnp.float32)
        filled = jnp.max(largest, axis=1, keepdims=True) > 0.0
        spread[place, :] = jnp.broadcast_to(jnp.where(filled, 1.0, 0.0), (own, LANES))
        token = by_row[pl.ds(pl.multiple_of(lax.bitwise_xor(me, number) * own, own), own), :]
        digits = jnp.where(
            lane == 0, token // 4096, jnp.where(lane == 1, token // 64 % 64, token % 64)
        )
        rows[place, depth:] = jnp.where(lane < 3, digits, 0).astype(jnp.float32).astype(jnp.bfloat16)

    filled = spread[...]
    row = lax.broadcasted_iota(jnp.int32, (n_rows, n_rows), 0)
    column = lax.broadcasted_iota(jnp.int32, (n_rows, n_rows), 1)
    earlier = (column < row).astype(jnp.float32).astype(jnp.bfloat16)
    position = jnp.dot(earlier, filled.astype(jnp.bfloat16), preferred_element_type=jnp.float32)
    n_filled = jnp.max(position + filled).astype(jnp.int32)
    position = jnp.where(filled > 0.0, position, -1.0).astype(jnp.int32)
    lane = lax.broadcasted_iota(jnp.int32, (n_rows, LANES), 1)
    for first in range(0, n_rows, LANES):
        hit = (position == lane + first).astype(jnp.float32)
        chosen[:, first : first + LANES] = hit.astype(jnp.bfloat16)
    across = (((0,), (0,)), ((), ()))
    for first in range(0, depth, 512):
        piece = slice(first, first + 512)
        packed[:, piece] = lax.dot_general(
            chosen[...], rows[:, piece], across, preferred_element_type=jnp.float32
        ).astype(jnp.bfloat16)
    digits = lax.dot_general(chosen[...], rows[:, depth:], across, preferred_element_type=jnp.float32)
    token = (digits[:, 0:1] * 4096.0 + digits[:, 1:2] * 64.0 + digits[:, 2:3]).astype(jnp.int32)
    wanted[...] = token - me * width - lane
    top[...] = jnp.full(top.shape, LOWEST, jnp.float32)
    for sums in (total, spread, picked):
        sums[...] = jnp.zeros(sums.shape, jnp.float32)

    def work(count):
        def multiply(index, slot):
            columns = pl.ds(pl.multiple_of(index * tile, tile), tile)
            logits[slot, :count] = jnp.dot(
                packed[:count, :], head[:, columns], preferred_element_type=jnp.float32
            )

        def collect(index, slot):
            step = 32
            for begin in range(0, count, step):
                place = slice(begin, min(begin + step, count))
                pieces = [logits[slot, place, c : c + LANES] for c in range(0, tile, LANES)]
                last = top[place]
                new = jnp.maximum(last, functools.reduce(jnp.maximum, pieces))
                shift = last - new
                factor = jnp.exp(shift)
                sums = total[place]
                spreads = (spread[place] + shift * sums) * factor
                sums = sums * factor
                found = picked[place]
                target = wanted[place]
                for number, piece in enumerate(pieces):
                    shifted = piece - new
                    power = jnp.exp(shifted)
                    sums = sums + power
                    spreads = spreads + power * shifted
                    found = jnp.where(target == index * tile + number * LANES, piece, found)
                top[place] = new
                total[place] = sums
                spread[place] = spreads
                picked[place] = found

        sweep(width // tile, multiply, collect)

    for fewer, count in zip((0,) + counts, counts):

        @pl.when((n_filled > fewer) & (n_filled <= count))
        def _():
            work(count)

    row_top = jnp.max(top[...], axis=1, keepdims=True)
    shift = top[...] - row_top
    factor = jnp.exp(shift)
    row_total = jnp.sum(total[...] * factor, axis=1, keepdims=True)
    row_spread = jnp.sum((spread[...] + shift * total[...]) * factor, axis=1, keepdims=True)
    row_picked = jnp.sum(picked[...], axis=1, keepdims=True)
    kind = lane % 4
    values = jnp.where(
        kind == 0,
        row_top,
        jnp.where(kind == 1, row_total, jnp.where(kind == 2, row_spread, row_picked)),
    )
    high = values.astype(jnp.bfloat16)
    rest = values - high.astype(jnp.float32)
    middle = rest.astype(jnp.bfloat16)
    low = (rest - middle.astype(jnp.float32)).astype(jnp.bfloat16)
    parts = jnp.where(
        lane < 4,
        high.astype(jnp.float32),
        jnp.where(lane < 8, middle.astype(jnp.float32), low.astype(jnp.float32)),
    ).astype(jnp.bfloat16)
    unpacked = jnp.dot(chosen[...], parts, preferred_element_type=jnp.float32)
    table = jnp.where(lane == 12, filled, unpacked).T
    sums = table[0:4] + table[4:8] + table[8:12]
    known = jnp.where(lax.broadcasted_iota(jnp.int32, sums.shape, 0) == 1, float(width), 0.0)
    sums = sums + known * (1.0 - table[12:13])
    kept_ref[...] = sums[:, : n_rows // 2]
    sent_ref[...] = sums[:, n_rows // 2 :]


def head_stats(blocks, tokens, head):
    own, depth = blocks[0].shape
    width = head.shape[1]
    tile = next(t for t in (1024, 1280, 512, 256, 128) if width % t == 0)
    n_rows = own * len(blocks)
    counts = tuple(n_rows * k // 8 for k in (4, 5, 6, 7, 8))
    args = [*blocks, tokens, pltpu.with_memory_space_constraint(head, pltpu.VMEM)]
    lanes = pltpu.VMEM((n_rows, LANES), jnp.float32)
    return pl.pallas_call(
        functools.partial(head_kernel, tile, counts),
        in_specs=[IN_VMEM] * len(args),
        out_specs=[IN_VMEM] * 2,
        out_shape=[jax.ShapeDtypeStruct((4, n_rows // 2), jnp.float32)] * 2,
        scratch_shapes=[
            pltpu.VMEM((n_rows, depth + LANES), jnp.bfloat16),
            pltpu.VMEM((n_rows, depth), jnp.bfloat16),
            pltpu.VMEM((n_rows, n_rows), jnp.bfloat16),
            pltpu.VMEM((2, n_rows, tile), jnp.float32),
            pltpu.VMEM((n_rows, LANES), jnp.int32),
            pltpu.VMEM((n_rows, LANES), jnp.int32),
            *[lanes] * 4,
        ],
        compiler_params=pltpu.CompilerParams(
            vmem_limit_bytes=n_rows * (6 * depth + 8 * tile + 8 * n_rows + 64 * LANES) + 2**22
        ),
        cost_estimate=pl.CostEstimate(flops=1, bytes_accessed=500 * 2**20, transcendentals=0),
    )(*args)


def merge(mine, theirs):
    top = jnp.maximum(mine[0], theirs[0])
    a, b = mine[0] - top, theirs[0] - top
    fa, fb = jnp.exp(a), jnp.exp(b)
    total = mine[1] * fa + theirs[1] * fb
    spread = (mine[2] + a * mine[1]) * fa + (theirs[2] + b * theirs[1]) * fb
    return jnp.stack([top, total, spread, mine[3] + theirs[3]])


def swap(array, distance, size):
    return lax.ppermute(array, "vocab", [(i, i ^ distance) for i in range(size)])


def gather(normed, size):
    blocks = {0: normed}
    for d in sorted(range(1, size), key=lambda d: (bin(d).count("1"), -d)):
        distance = d & -d if d % 4 != 3 or d < 4 else 2
        if d == size // 2 + size // 4:
            direct = [1 << k for k in range(size.bit_length() - 1)]
            for k, block in zip(direct, lax.optimization_barrier(tuple(blocks[k] for k in direct))):
                blocks[k] = block
        blocks[d] = swap(blocks[d ^ distance], distance, size)
    return [blocks[d] for d in range(size)]


def per_device(size, hidden_rows, norm_gain, head_weight, token_ids, live_count):
    own = hidden_rows.shape[0]
    tokens = token_ids[None, :]
    normed, live = norm_rows(hidden_rows, norm_gain[None, :], live_count[None, :])
    kept, sent = head_stats(gather(normed, size), tokens, head_weight)
    distance = size // 2
    while True:
        stats = merge(kept, swap(sent, distance, size))
        distance //= 2
        if not distance:
            break
        kept, sent = stats[:, : distance * own], stats[:, distance * own :]
    top, total, spread, picked = lax.optimization_barrier(tuple(stats))
    log_total = jnp.log(total)
    logprob = picked - top - log_total
    entropy = log_total - spread / total
    live = live[0] > 0.0
    return jnp.where(live, logprob, 0.0), jnp.where(live, entropy, 0.0)


def solution(mesh):
    placed = (P(("req", "vocab"), None), P(), P(None, "vocab"), P("req"), P(("req", "vocab")))
    return jax.shard_map(
        functools.partial(per_device, mesh.shape["vocab"]),
        mesh=mesh,
        in_specs=placed,
        out_specs=(P(("req", "vocab")), P(("req", "vocab"))),
        check_vma=False,
    )
```

```python
import functools

import jax
import jax.numpy as jnp
from jax import lax
from jax.experimental import pallas as pl
from jax.experimental.pallas import tpu as pltpu
from jax.sharding import PartitionSpec as P

LANES = 128
LOWEST = -1e30
IN_VMEM = pl.BlockSpec(memory_space=pltpu.VMEM)
ANYWHERE = pl.BlockSpec(memory_space=pl.ANY)


def normalise(values, gain):
    values = values.astype(jnp.float32)
    squares = jnp.mean(values * values, axis=1, keepdims=True)
    return values * lax.rsqrt(squares + 1e-06) * gain


def norm_kernel(hidden_hbm, gain_hbm, count, out_ref, live_ref, hidden, gain, sems):
    copies = [
        pltpu.make_async_copy(source, target, sems.at[number])
        for number, (source, target) in enumerate(((hidden_hbm, hidden), (gain_hbm, gain)))
    ]
    for copy in copies:
        copy.start()
    for copy in copies:
        copy.wait()
    row = lax.broadcasted_iota(jnp.int32, hidden.shape, 0)
    alive = row < jnp.broadcast_to(count[...], hidden.shape)
    out_ref[...] = jnp.where(alive, normalise(hidden[...], gain[...]), 0.0).astype(jnp.bfloat16)
    column = lax.broadcasted_iota(jnp.int32, live_ref.shape, 1)
    live_ref[...] = (column < jnp.broadcast_to(count[...], live_ref.shape)).astype(jnp.float32)


def norm_rows(hidden_rows, gain, live_count):
    args = (hidden_rows, gain, live_count)
    return pl.pallas_call(
        norm_kernel,
        in_specs=[ANYWHERE, ANYWHERE, IN_VMEM],
        out_specs=[IN_VMEM] * 2,
        out_shape=[
            jax.ShapeDtypeStruct(hidden_rows.shape, jnp.bfloat16),
            jax.ShapeDtypeStruct((1, hidden_rows.shape[0]), jnp.float32),
        ],
        scratch_shapes=[pltpu.VMEM(x.shape, x.dtype) for x in args[:2]] + [pltpu.SemaphoreType.DMA((2,))],
        compiler_params=pltpu.CompilerParams(vmem_limit_bytes=3 * 2**20),
        cost_estimate=pl.CostEstimate(flops=10**11, bytes_accessed=10**8, transcendentals=0),
    )(*(pltpu.with_memory_space_constraint(x, pltpu.HBM) for x in args[:2]), live_count)


def column_of(tokens):
    wide = jnp.broadcast_to(tokens.astype(jnp.float32), (LANES, tokens.shape[1]))
    return wide.T.astype(jnp.int32)


def sweep(n_tiles, multiply, collect):
    multiply(0, 0)
    pairs = (n_tiles - 1) // 2

    @pl.loop(0, pairs, unroll=4 if pairs % 4 == 0 else 1)
    def _(pair):
        tile = pair * 2
        multiply(tile + 1, 1)
        collect(tile, 0)
        multiply(tile + 2, 0)
        collect(tile + 1, 1)

    if n_tiles % 2:
        collect(n_tiles - 1, 0)
    else:
        multiply(n_tiles - 1, 1)
        collect(n_tiles - 2, 0)
        collect(n_tiles - 1, 1)


def head_kernel(tile, counts, *refs):
    n_blocks = len(refs) - 14
    blocks, refs = refs[:n_blocks], refs[n_blocks:]
    token_ref, head, kept_ref, sent_ref, rows, packed, chosen, logits, wanted, by_row = refs[:10]
    top, total, spread, picked = refs[10:]
    own, depth = blocks[0].shape
    width = head.shape[1]
    me = lax.axis_index("vocab")
    n_rows = n_blocks * own

    by_row[...] = column_of(token_ref[...])
    lane = lax.broadcasted_iota(jnp.int32, (own, LANES), 1)
    for number, block in enumerate(blocks):
        place = slice(number * own, (number + 1) * own)
        values = block[...]
        rows[place, :depth] = values
        pieces = [jnp.abs(values[:, c : c + LANES]) for c in range(0, depth, LANES)]
        largest = functools.reduce(jnp.maximum, pieces).astype(jnp.float32)
        filled = jnp.max(largest, axis=1, keepdims=True) > 0.0
        spread[place, :] = jnp.broadcast_to(jnp.where(filled, 1.0, 0.0), (own, LANES))
        token = by_row[pl.ds(pl.multiple_of(lax.bitwise_xor(me, number) * own, own), own), :]
        digits = jnp.where(
            lane == 0, token >> 12, jnp.where(lane == 1, (token >> 6) & 63, token & 63)
        )
        rows[place, depth:] = jnp.where(lane < 3, digits, 0).astype(jnp.float32).astype(jnp.bfloat16)

    filled = spread[...]
    row = lax.broadcasted_iota(jnp.int32, (n_rows, n_rows), 0)
    column = lax.broadcasted_iota(jnp.int32, (n_rows, n_rows), 1)
    earlier = (column < row).astype(jnp.float32).astype(jnp.bfloat16)
    position = jnp.dot(earlier, filled.astype(jnp.bfloat16), preferred_element_type=jnp.float32)
    n_filled = jnp.max(position + filled).astype(jnp.int32)
    position = jnp.where(filled > 0.0, position, -1.0).astype(jnp.int32)
    lane = lax.broadcasted_iota(jnp.int32, (n_rows, LANES), 1)
    for first in range(0, n_rows, LANES):
        hit = (position == lane + first).astype(jnp.float32)
        chosen[:, first : first + LANES] = hit.astype(jnp.bfloat16)
    spot = position.astype(jnp.float32).T[0:1, :].astype(jnp.int32)
    packing = (row == jnp.broadcast_to(spot, row.shape)).astype(jnp.float32).astype(jnp.bfloat16)
    for first in range(0, depth, 512):
        piece = slice(first, first + 512)
        packed[:, piece] = jnp.dot(
            packing, rows[:, piece], preferred_element_type=jnp.float32
        ).astype(jnp.bfloat16)
    digits = jnp.dot(packing, rows[:, depth:], preferred_element_type=jnp.float32)
    token = (digits[:, 0:1] * 4096.0 + digits[:, 1:2] * 64.0 + digits[:, 2:3]).astype(jnp.int32)
    wanted[...] = token - me * width - lane
    top[...] = jnp.full(top.shape, LOWEST, jnp.float32)
    for sums in (total, spread, picked):
        sums[...] = jnp.zeros(sums.shape, jnp.float32)

    def work(count):
        def multiply(index, slot):
            columns = pl.ds(pl.multiple_of(index * tile, tile), tile)
            logits[slot, :count] = jnp.dot(
                packed[:count, :], head[:, columns], preferred_element_type=jnp.float32
            )

        def collect(index, slot):
            step = 32
            for begin in range(0, count, step):
                place = slice(begin, min(begin + step, count))
                pieces = [logits[slot, place, c : c + LANES] for c in range(0, tile, LANES)]
                last = top[place]
                new = jnp.maximum(last, functools.reduce(jnp.maximum, pieces))
                shift = last - new
                factor = jnp.exp(shift)
                sums = total[place]
                spreads = (spread[place] + shift * sums) * factor
                sums = sums * factor
                found = picked[place]
                target = wanted[place]
                for number, piece in enumerate(pieces):
                    shifted = piece - new
                    power = jnp.exp(shifted)
                    sums = sums + power
                    spreads = spreads + power * shifted
                    found = jnp.where(target == index * tile + number * LANES, piece, found)
                top[place] = new
                total[place] = sums
                spread[place] = spreads
                picked[place] = found

        sweep(width // tile, multiply, collect)

    for fewer, count in zip((0,) + counts, counts):

        @pl.when((n_filled > fewer) & (n_filled <= count))
        def _():
            work(count)

    row_top = jnp.max(top[...], axis=1, keepdims=True)
    shift = top[...] - row_top
    factor = jnp.exp(shift)
    row_total = jnp.sum(total[...] * factor, axis=1, keepdims=True)
    row_spread = jnp.sum((spread[...] + shift * total[...]) * factor, axis=1, keepdims=True)
    row_picked = jnp.sum(picked[...], axis=1, keepdims=True)
    kind = lane % 4
    values = jnp.where(
        kind == 0,
        row_top,
        jnp.where(kind == 1, row_total, jnp.where(kind == 2, row_spread, row_picked)),
    )
    high = values.astype(jnp.bfloat16)
    rest = values - high.astype(jnp.float32)
    middle = rest.astype(jnp.bfloat16)
    low = (rest - middle.astype(jnp.float32)).astype(jnp.bfloat16)
    parts = jnp.where(
        lane < 4,
        high.astype(jnp.float32),
        jnp.where(lane < 8, middle.astype(jnp.float32), low.astype(jnp.float32)),
    ).astype(jnp.bfloat16)
    unpacked = jnp.dot(chosen[...], parts, preferred_element_type=jnp.float32)
    table = jnp.where(lane == 12, filled, unpacked).T
    sums = table[0:4] + table[4:8] + table[8:12]
    known = jnp.where(lax.broadcasted_iota(jnp.int32, sums.shape, 0) == 1, float(width), 0.0)
    sums = sums + known * (1.0 - table[12:13])
    kept_ref[...] = sums[:, : n_rows // 2]
    sent_ref[...] = sums[:, n_rows // 2 :]


def head_stats(blocks, tokens, head):
    own, depth = blocks[0].shape
    width = head.shape[1]
    tile = next(t for t in (1024, 1280, 512, 256, 128) if width % t == 0)
    n_rows = own * len(blocks)
    counts = tuple(n_rows * k // 8 for k in (4, 5, 6, 8))
    args = [*blocks, tokens, pltpu.with_memory_space_constraint(head, pltpu.VMEM)]
    lanes = pltpu.VMEM((n_rows, LANES), jnp.float32)
    return pl.pallas_call(
        functools.partial(head_kernel, tile, counts),
        in_specs=[IN_VMEM] * len(args),
        out_specs=[IN_VMEM] * 2,
        out_shape=[jax.ShapeDtypeStruct((4, n_rows // 2), jnp.float32)] * 2,
        scratch_shapes=[
            pltpu.VMEM((n_rows, depth + LANES), jnp.bfloat16),
            pltpu.VMEM((n_rows, depth), jnp.bfloat16),
            pltpu.VMEM((n_rows, n_rows), jnp.bfloat16),
            pltpu.VMEM((2, n_rows, tile), jnp.float32),
            pltpu.VMEM((n_rows, LANES), jnp.int32),
            pltpu.VMEM((n_rows, LANES), jnp.int32),
            *[lanes] * 4,
        ],
        compiler_params=pltpu.CompilerParams(
            vmem_limit_bytes=n_rows * (6 * depth + 8 * tile + 8 * n_rows + 64 * LANES) + 2**22
        ),
        cost_estimate=pl.CostEstimate(flops=1, bytes_accessed=500 * 2**20, transcendentals=0),
    )(*args)


def merge(mine, theirs):
    top = jnp.maximum(mine[0], theirs[0])
    a, b = mine[0] - top, theirs[0] - top
    fa, fb = jnp.exp(a), jnp.exp(b)
    total = mine[1] * fa + theirs[1] * fb
    spread = (mine[2] + a * mine[1]) * fa + (theirs[2] + b * theirs[1]) * fb
    return jnp.stack([top, total, spread, mine[3] + theirs[3]])


def swap(array, distance, size):
    return lax.ppermute(array, "vocab", [(i, i ^ distance) for i in range(size)])


def gather(normed, size):
    blocks = {0: normed}
    for d in sorted(range(1, size), key=lambda d: (bin(d).count("1"), -d)):
        distance = d & -d if d % 4 != 3 or d < 4 else 2
        if d == size // 2 + size // 4:
            direct = [1 << k for k in range(size.bit_length() - 1)]
            for k, block in zip(direct, lax.optimization_barrier(tuple(blocks[k] for k in direct))):
                blocks[k] = block
        blocks[d] = swap(blocks[d ^ distance], distance, size)
    return [blocks[d] for d in range(size)]


def per_device(size, hidden_rows, norm_gain, head_weight, token_ids, live_count):
    own = hidden_rows.shape[0]
    tokens = token_ids[None, :]
    normed, live = norm_rows(hidden_rows, norm_gain[None, :], live_count[None, :])
    kept, sent = head_stats(gather(normed, size), tokens, head_weight)
    distance = size // 2
    while True:
        stats = merge(kept, swap(sent, distance, size))
        distance //= 2
        if not distance:
            break
        kept, sent = stats[:, : distance * own], stats[:, distance * own :]
    top, total, spread, picked = lax.optimization_barrier(tuple(stats))
    log_total = jnp.log(total)
    logprob = picked - top - log_total
    entropy = log_total - spread / total
    live = live[0] > 0.0
    return jnp.where(live, logprob, 0.0), jnp.where(live, entropy, 0.0)


def solution(mesh):
    placed = (P(("req", "vocab"), None), P(), P(None, "vocab"), P("req"), P(("req", "vocab")))
    return jax.shard_map(
        functools.partial(per_device, mesh.shape["vocab"]),
        mesh=mesh,
        in_specs=placed,
        out_specs=(P(("req", "vocab")), P(("req", "vocab"))),
        check_vma=False,
    )
```

```python
import functools

import jax
import jax.numpy as jnp
from jax import lax
from jax.experimental import pallas as pl
from jax.experimental.pallas import tpu as pltpu
from jax.sharding import PartitionSpec as P

LANES = 128
LOWEST = -1e30
IN_VMEM = pl.BlockSpec(memory_space=pltpu.VMEM)
ANYWHERE = pl.BlockSpec(memory_space=pl.ANY)


def normalise(values, gain):
    values = values.astype(jnp.float32)
    squares = jnp.mean(values * values, axis=1, keepdims=True)
    return values * lax.rsqrt(squares + 1e-06) * gain


def norm_kernel(hidden_hbm, gain_hbm, count, out_ref, live_ref, hidden, gain, sems):
    copies = [
        pltpu.make_async_copy(source, target, sems.at[number])
        for number, (source, target) in enumerate(((hidden_hbm, hidden), (gain_hbm, gain)))
    ]
    for copy in copies:
        copy.start()
    for copy in copies:
        copy.wait()
    row = lax.broadcasted_iota(jnp.int32, hidden.shape, 0)
    alive = row < jnp.broadcast_to(count[...], hidden.shape)
    out_ref[...] = jnp.where(alive, normalise(hidden[...], gain[...]), 0.0).astype(jnp.bfloat16)
    column = lax.broadcasted_iota(jnp.int32, live_ref.shape, 1)
    live_ref[...] = (column < jnp.broadcast_to(count[...], live_ref.shape)).astype(jnp.float32)


def norm_rows(hidden_rows, gain, live_count):
    args = (hidden_rows, gain, live_count)
    return pl.pallas_call(
        norm_kernel,
        in_specs=[ANYWHERE, ANYWHERE, IN_VMEM],
        out_specs=[IN_VMEM] * 2,
        out_shape=[
            jax.ShapeDtypeStruct(hidden_rows.shape, jnp.bfloat16),
            jax.ShapeDtypeStruct((1, hidden_rows.shape[0]), jnp.float32),
        ],
        scratch_shapes=[pltpu.VMEM(x.shape, x.dtype) for x in args[:2]] + [pltpu.SemaphoreType.DMA((2,))],
        compiler_params=pltpu.CompilerParams(vmem_limit_bytes=3 * 2**20),
        cost_estimate=pl.CostEstimate(flops=10**11, bytes_accessed=10**8, transcendentals=0),
    )(*(pltpu.with_memory_space_constraint(x, pltpu.HBM) for x in args[:2]), live_count)


def column_of(tokens):
    wide = jnp.broadcast_to(tokens.astype(jnp.float32), (LANES, tokens.shape[1]))
    return wide.T.astype(jnp.int32)


def sweep(n_tiles, multiply, collect):
    multiply(0, 0)
    pairs = (n_tiles - 1) // 2

    @pl.loop(0, pairs, unroll=4 if pairs % 4 == 0 else 1)
    def _(pair):
        tile = pair * 2
        multiply(tile + 1, 1)
        collect(tile, 0)
        multiply(tile + 2, 0)
        collect(tile + 1, 1)

    if n_tiles % 2:
        collect(n_tiles - 1, 0)
    else:
        multiply(n_tiles - 1, 1)
        collect(n_tiles - 2, 0)
        collect(n_tiles - 1, 1)


def head_kernel(tile, counts, *refs):
    n_blocks = len(refs) - 14
    blocks, refs = refs[:n_blocks], refs[n_blocks:]
    token_ref, head, kept_ref, sent_ref, rows, packed, chosen, logits, wanted, by_row = refs[:10]
    top, total, spread, picked = refs[10:]
    own, depth = blocks[0].shape
    width = head.shape[1]
    me = lax.axis_index("vocab")
    n_rows = n_blocks * own

    by_row[...] = column_of(token_ref[...])
    lane = lax.broadcasted_iota(jnp.int32, (own, LANES), 1)
    for number, block in enumerate(blocks):
        place = slice(number * own, (number + 1) * own)
        values = block[...]
        rows[place, :depth] = values
        pieces = [jnp.abs(values[:, c : c + LANES]) for c in range(0, depth, LANES)]
        largest = functools.reduce(jnp.maximum, pieces).astype(jnp.float32)
        filled = jnp.max(largest, axis=1, keepdims=True) > 0.0
        spread[place, :] = jnp.broadcast_to(jnp.where(filled, 1.0, 0.0), (own, LANES))
        token = by_row[pl.ds(pl.multiple_of(lax.bitwise_xor(me, number) * own, own), own), :]
        digits = jnp.where(
            lane == 0, token >> 12, jnp.where(lane == 1, (token >> 6) & 63, token & 63)
        )
        rows[place, depth:] = jnp.where(lane < 3, digits, 0).astype(jnp.float32).astype(jnp.bfloat16)

    filled = spread[...]
    row = lax.broadcasted_iota(jnp.int32, (n_rows, n_rows), 0)
    column = lax.broadcasted_iota(jnp.int32, (n_rows, n_rows), 1)
    earlier = (column < row).astype(jnp.float32).astype(jnp.bfloat16)
    position = jnp.dot(earlier, filled.astype(jnp.bfloat16), preferred_element_type=jnp.float32)
    n_filled = jnp.max(position + filled).astype(jnp.int32)
    position = jnp.where(filled > 0.0, position, -1.0).astype(jnp.int32)
    lane = lax.broadcasted_iota(jnp.int32, (n_rows, LANES), 1)
    for first in range(0, n_rows, LANES):
        hit = (position == lane + first).astype(jnp.float32)
        chosen[:, first : first + LANES] = hit.astype(jnp.bfloat16)
    spot = position.astype(jnp.float32).T[0:1, :].astype(jnp.int32)
    packing = (row == jnp.broadcast_to(spot, row.shape)).astype(jnp.float32).astype(jnp.bfloat16)
    for first in range(0, depth, 512):
        piece = slice(first, first + 512)
        packed[:, piece] = jnp.dot(
            packing, rows[:, piece], preferred_element_type=jnp.float32
        ).astype(jnp.bfloat16)
    digits = jnp.dot(packing, rows[:, depth:], preferred_element_type=jnp.float32)
    token = (digits[:, 0:1] * 4096.0 + digits[:, 1:2] * 64.0 + digits[:, 2:3]).astype(jnp.int32)
    wanted[...] = token - me * width - lane
    top[...] = jnp.full(top.shape, LOWEST, jnp.float32)
    for sums in (total, spread, picked):
        sums[...] = jnp.zeros(sums.shape, jnp.float32)

    def work(count):
        def multiply(index, slot):
            columns = pl.ds(pl.multiple_of(index * tile, tile), tile)
            logits[slot, :count] = jnp.dot(
                packed[:count, :], head[:, columns], preferred_element_type=jnp.float32
            )

        def collect(index, slot):
            step = 16
            for begin in range(0, count, step):
                place = slice(begin, min(begin + step, count))
                pieces = [logits[slot, place, c : c + LANES] for c in range(0, tile, LANES)]
                last = top[place]
                new = jnp.maximum(last, functools.reduce(jnp.maximum, pieces))
                shift = last - new
                factor = jnp.exp(shift)
                sums = total[place]
                spreads = (spread[place] + shift * sums) * factor
                sums = sums * factor
                found = picked[place]
                target = wanted[place]
                for number, piece in enumerate(pieces):
                    shifted = piece - new
                    power = jnp.exp(shifted)
                    sums = sums + power
                    spreads = spreads + power * shifted
                    found = jnp.where(target == index * tile + number * LANES, piece, found)
                top[place] = new
                total[place] = sums
                spread[place] = spreads
                picked[place] = found

        sweep(width // tile, multiply, collect)

    for fewer, count in zip((0,) + counts, counts):

        @pl.when((n_filled > fewer) & (n_filled <= count))
        def _():
            work(count)

    row_top = jnp.max(top[...], axis=1, keepdims=True)
    shift = top[...] - row_top
    factor = jnp.exp(shift)
    row_total = jnp.sum(total[...] * factor, axis=1, keepdims=True)
    row_spread = jnp.sum((spread[...] + shift * total[...]) * factor, axis=1, keepdims=True)
    row_picked = jnp.sum(picked[...], axis=1, keepdims=True)
    kind = lane % 4
    values = jnp.where(
        kind == 0,
        row_top,
        jnp.where(kind == 1, row_total, jnp.where(kind == 2, row_spread, row_picked)),
    )
    high = values.astype(jnp.bfloat16)
    rest = values - high.astype(jnp.float32)
    middle = rest.astype(jnp.bfloat16)
    low = (rest - middle.astype(jnp.float32)).astype(jnp.bfloat16)
    parts = jnp.where(
        lane < 4,
        high.astype(jnp.float32),
        jnp.where(lane < 8, middle.astype(jnp.float32), low.astype(jnp.float32)),
    ).astype(jnp.bfloat16)
    unpacked = jnp.dot(chosen[...], parts, preferred_element_type=jnp.float32)
    table = jnp.where(lane == 12, filled, unpacked).T
    sums = table[0:4] + table[4:8] + table[8:12]
    known = jnp.where(lax.broadcasted_iota(jnp.int32, sums.shape, 0) == 1, float(width), 0.0)
    sums = sums + known * (1.0 - table[12:13])
    kept_ref[...] = sums[:, : n_rows // 2]
    sent_ref[...] = sums[:, n_rows // 2 :]


def head_stats(blocks, tokens, head):
    own, depth = blocks[0].shape
    width = head.shape[1]
    tile = next(t for t in (1024, 1280, 512, 256, 128) if width % t == 0)
    n_rows = own * len(blocks)
    counts = tuple(n_rows * k // 8 for k in (4, 5, 6, 8))
    args = [*blocks, tokens, pltpu.with_memory_space_constraint(head, pltpu.VMEM)]
    lanes = pltpu.VMEM((n_rows, LANES), jnp.float32)
    return pl.pallas_call(
        functools.partial(head_kernel, tile, counts),
        in_specs=[IN_VMEM] * len(args),
        out_specs=[IN_VMEM] * 2,
        out_shape=[jax.ShapeDtypeStruct((4, n_rows // 2), jnp.float32)] * 2,
        scratch_shapes=[
            pltpu.VMEM((n_rows, depth + LANES), jnp.bfloat16),
            pltpu.VMEM((n_rows, depth), jnp.bfloat16),
            pltpu.VMEM((n_rows, n_rows), jnp.bfloat16),
            pltpu.VMEM((2, n_rows, tile), jnp.float32),
            pltpu.VMEM((n_rows, LANES), jnp.int32),
            pltpu.VMEM((n_rows, LANES), jnp.int32),
            *[lanes] * 4,
        ],
        compiler_params=pltpu.CompilerParams(
            vmem_limit_bytes=n_rows * (6 * depth + 8 * tile + 8 * n_rows + 64 * LANES) + 2**22
        ),
        cost_estimate=pl.CostEstimate(flops=1, bytes_accessed=500 * 2**20, transcendentals=0),
    )(*args)


def merge(mine, theirs):
    top = jnp.maximum(mine[0], theirs[0])
    a, b = mine[0] - top, theirs[0] - top
    fa, fb = jnp.exp(a), jnp.exp(b)
    total = mine[1] * fa + theirs[1] * fb
    spread = (mine[2] + a * mine[1]) * fa + (theirs[2] + b * theirs[1]) * fb
    return jnp.stack([top, total, spread, mine[3] + theirs[3]])


def swap(array, distance, size):
    return lax.ppermute(array, "vocab", [(i, i ^ distance) for i in range(size)])


def gather(normed, size):
    blocks = {0: normed}
    for d in sorted(range(1, size), key=lambda d: (bin(d).count("1"), -d)):
        distance = d & -d if d % 4 != 3 or d < 4 else 2
        if d == size // 2 + size // 4:
            direct = [1 << k for k in range(size.bit_length() - 1)]
            for k, block in zip(direct, lax.optimization_barrier(tuple(blocks[k] for k in direct))):
                blocks[k] = block
        blocks[d] = swap(blocks[d ^ distance], distance, size)
    return [blocks[d] for d in range(size)]


def per_device(size, hidden_rows, norm_gain, head_weight, token_ids, live_count):
    own = hidden_rows.shape[0]
    tokens = token_ids[None, :]
    normed, live = norm_rows(hidden_rows, norm_gain[None, :], live_count[None, :])
    kept, sent = head_stats(gather(normed, size), tokens, head_weight)
    distance = size // 2
    while True:
        stats = merge(kept, swap(sent, distance, size))
        distance //= 2
        if not distance:
            break
        kept, sent = stats[:, : distance * own], stats[:, distance * own :]
    top, total, spread, picked = lax.optimization_barrier(tuple(stats))
    log_total = jnp.log(total)
    logprob = picked - top - log_total
    entropy = log_total - spread / total
    live = live[0] > 0.0
    return jnp.where(live, logprob, 0.0), jnp.where(live, entropy, 0.0)


def solution(mesh):
    placed = (P(("req", "vocab"), None), P(), P(None, "vocab"), P("req"), P(("req", "vocab")))
    return jax.shard_map(
        functools.partial(per_device, mesh.shape["vocab"]),
        mesh=mesh,
        in_specs=placed,
        out_specs=(P(("req", "vocab")), P(("req", "vocab"))),
        check_vma=False,
    )
```
